32 devices in a mesh: lat: 4 (over y, x), lon: 2 (over core), obs: 4 (over z).
Axes of the slice: x: 2, y: 2, z: 4, core: 2. Of those that a mesh axis runs over, the one named last changes fastest.
Arguments:
- coords: bfloat16 [2048, 2, 256], P(('lat', 'lon', 'obs')), may hold values from 0 to 1
- values: bfloat16 [2048, 8, 256], P(('lat', 'lon', 'obs')), may hold values from -6 to 6
- live: int32 [2048, 256], P(('lat', 'lon', 'obs')), may hold values 0 or 1
- tile_of: int32 [2048, 1], P(('lat', 'lon', 'obs')), may hold values from 0 to 7; in each aligned block of 64 rows (0 to 63, 64 to 127, ...) at most 16 rows name the same one
- lengthscale: float32 [9], replicated, may hold values from 0.7 to 6
- w_in: float32 [9, 256], replicated, may hold values from -0.3 to 0.3
- w_conv: bfloat16 [3, 3, 256, 256], replicated, may hold values from -0.125 to 0.125
- grad_out: bfloat16 [128, 256, 256], P(('lat', 'obs'), 'lon'), may hold values from -6 to 6
Outputs:
- grad_conv: float32 [3, 3, 256, 256], replicated
- grad_in: float32 [9, 256], replicated
- grad_values: float32 [2048, 8, 256], P(('lat', 'lon', 'obs'))
The draws below stay inside these ranges and needn't reach their ends.
Inputs may be any that keep to these rules, and one draw needn't show every extreme that they name: `tile_of`: in the rows of one device at most 16 blocks name the same tile, a bound that some block reaches. `live`: 1 marks an observation, 0 a padding slot.
All inputs are finite; a program needn't handle non-finite values. No bound on the sum of `live` on one device may be relied on, other than what follows from the above.
Results may differ from the reference program's by a relative error of at most 0.0031.
Values may be sent and summed in bfloat16 or wider, within the bound.
A program may use at most 64 MiB of HBM per device.

```python
import math
import jax
import jax.numpy as jnp
import numpy as np
from jax import lax

RD = 8
TW = 128
NB_DEV = 64
CH = 256
VARS = 8
OBS = 256
NLAT = 128
NLON = 256
CAP = 16
BLOCKS = 2048
N_LAT = 4
N_LON = 2
N_OBS = 4


def draw_values(key, part):
    key = jax.random.fold_in(key, 11)
    noise_key, offset_key = jax.random.split(key)
    noise_part = jax.random.normal(noise_key, (BLOCKS, VARS, OBS), jnp.float32)
    offset_part = 0.5 * jax.random.normal(offset_key, (1, VARS, 1), jnp.float32)
    return jnp.clip(noise_part + offset_part, -6.0, 6.0).astype(jnp.bfloat16)


def draw_grad_out(key, part):
    key = jax.random.fold_in(key, 13)
    noise_key, offset_key = jax.random.split(key)
    noise_part = jax.random.normal(noise_key, (NLAT, NLON, CH), jnp.float32)
    offset_part = 0.5 * jax.random.normal(offset_key, (1, 1, CH), jnp.float32)
    return jnp.clip(noise_part + offset_part, -6.0, 6.0).astype(jnp.bfloat16)


def place_ends(result, key, smallest, top_value):
    longest = result.shape.index(max(result.shape))
    spots = []
    for shift in (0, 1):
        where = [jax.random.randint(jax.random.fold_in(key, axis), (), 0, length) for axis, length in enumerate(result.shape)]
        where[longest] = (where[longest] + shift) % result.shape[longest]
        spots.append(tuple(where))
    return result.at[spots[0]].set(smallest).at[spots[1]].set(top_value)


def shard_levels(rng, extent, cuts, low, top_value):
    level, own = 1.0, jax.random.fold_in(rng, 6)
    for position, parts in cuts:
        steps = jnp.exp(jax.random.uniform(jax.random.fold_in(own, position), (parts,), jnp.float32, low / len(cuts), top_value / len(cuts)))
        level = level * jnp.repeat(steps, extent[position] // parts).reshape([-1 if axis == position else 1 for axis in range(len(extent))])
    return level


def deal_out(key, own, number, rows, amount, top, limit, lean):
    order = jax.random.permutation(key, amount)
    packed, usual = load_shares(amount, rows * top, limit, lean, True), load_shares(amount, rows * top, limit, lean, False)
    places = jnp.arange(amount)

    def named(sizes, rotation):
        used = int((sizes > 0).sum())
        fixed = max(1, used // 4)
        passed = fixed + (places - fixed + rotation * (used - fixed)) % max(1, amount - fixed)
        return jnp.zeros((amount,), jnp.int32).at[order[jnp.where(places < fixed, places, passed)]].set(jnp.asarray(sizes, jnp.int32))

    sizes = jnp.where(number % 4 == 0, named(packed, number // 4), named(usual, number - number // 4 - 1))
    mixed = jax.random.permutation(jax.random.fold_in(own, 3), amount)
    giver, taker = mixed[0:amount // 2 * 2:2], mixed[1:amount // 2 * 2:2]
    room = jnp.minimum(sizes[giver] - 1, limit - sizes[taker]) // 2
    room = jnp.where((giver == order[0]) | (taker == order[0]) | (sizes[taker] == 0), 0, jnp.maximum(room, 0))
    passed = jax.random.randint(jax.random.fold_in(own, 4), (amount // 2,), 0, 1 << 20) % (room + 1)
    sizes = sizes.at[giver].add(-passed).at[taker].add(passed)
    labels = jnp.searchsorted(jnp.cumsum(sizes), jnp.arange(rows * top), side="right").astype(jnp.int32)
    table = labels.reshape(top, rows).T
    table = table[jax.random.permutation(jax.random.fold_in(own, 1), rows)]
    rotation = jax.random.randint(jax.random.fold_in(own, 2), (rows, 1), 0, top)
    return jnp.take_along_axis(table, (jnp.arange(top)[None, :] + rotation) % top, axis=1)


def load_shares(amount, total, reach, lean, full):
    weights = [(1 << 20) // math.isqrt(rank ** lean) + 1 for rank in range(1, amount + 1)]
    largest = reach if full else min(reach, max(-(-total // amount), total * weights[0] // sum(weights)))
    least = 1 if total - largest >= amount - 1 else 0
    holding, rest = [largest] + [least] * (amount - 1), total - largest - least * (amount - 1)
    while rest > 0:
        free = [i for i in range(1, amount) if holding[i] < largest] or [i for i in range(1, amount) if holding[i] < reach]
        mass, left = sum([weights[i] for i in free]), rest
        for i in free:
            addition = min(reach - holding[i], max(1, left * weights[i] // mass), rest)
            holding[i] = holding[i] + addition
            rest = rest - addition
    return np.array(holding)


def normal_values(key, shape, width, most, kind=jnp.bfloat16):
    values = jax.random.normal(key, shape, jnp.float32) * width
    return jnp.minimum(jnp.maximum(values, -most), most).astype(kind)


def setup_inputs(seed: int = 0) -> dict:
    arg_keys = jax.random.split(jax.random.key(seed), 9)
    coords = jnp.clip(1.0 * jax.random.uniform(arg_keys[0], (BLOCKS, 2, OBS), jnp.float32) ** shard_levels(arg_keys[0], (BLOCKS, 2, OBS), ((0, 32),), -0.2, 0.2), 0.0, 1.0).astype(jnp.bfloat16)
    values = draw_values(jax.random.fold_in(arg_keys[8], 71), 0)
    live = place_ends((jax.random.randint(arg_keys[2], (BLOCKS, OBS), 0, 4) < 3).astype(jnp.int32), jax.random.fold_in(arg_keys[2], 1), 0, 1)
    tile_of_keys = jax.random.split(jax.random.fold_in(arg_keys[3], 1), BLOCKS // NB_DEV)
    tile_of_turns = jax.random.permutation(jax.random.fold_in(arg_keys[3], 3), BLOCKS // NB_DEV)
    tile_of = jax.vmap(lambda own, number: deal_out(jax.random.fold_in(arg_keys[3], 2), own, number, NB_DEV, N_LAT * N_LON, 1, CAP, 2))(tile_of_keys, tile_of_turns).reshape((BLOCKS, 1))
    lengthscale = jnp.clip(jnp.exp(jax.random.uniform(arg_keys[4], (VARS + 1,), jnp.float32, math.log(0.7), math.log(6.0))), 0.7, 6.0)
    w_in = normal_values(arg_keys[5], (VARS + 1, CH), 0.05, 0.3, jnp.float32)
    w_conv = normal_values(arg_keys[6], (3, 3, CH, CH), (9 * CH) ** -0.5, 0.125)
    grad_out = draw_grad_out(jax.random.fold_in(arg_keys[8], 71), 0)
    return dict(coords=coords, values=values, live=live, tile_of=tile_of, lengthscale=lengthscale, w_in=w_in, w_conv=w_conv, grad_out=grad_out)


blocks_per_step = 8


def kernel_rows(positions, count, scales):
    centers = jnp.arange(count, dtype=jnp.float32) + 0.5
    diff = centers[:, None] - positions[..., None, :]
    inverse = 1.0 / (2.0 * scales * scales)
    square = diff * diff
    return jnp.exp(-square[..., None, :, :] * inverse[:, None, None])


def rounded(field):
    return lax.optimization_barrier(field.astype(jnp.bfloat16)).astype(jnp.float32)


def pad_grid(field):
    wrapped = jnp.concatenate([field[:, -1:], field, field[:, :1]], axis=1)
    return jnp.pad(wrapped, ((1, 1), (0, 0), (0, 0)))


def reference(coords, values, live, tile_of, lengthscale, w_in, w_conv, grad_out):
    tiles = N_LAT * N_LON
    tile_rows = RD * N_OBS
    tile_cols = TW
    total_blocks = coords.shape[0]
    live_mask = live.astype(jnp.bfloat16)
    weighted = jnp.concatenate([values * live_mask[:, None, :], live_mask[:, None, :]], axis=1)
    steps_count = total_blocks // blocks_per_step
    tile_ids = jnp.arange(tiles, dtype=jnp.int32)

    def pieces(index):
        start = (index * blocks_per_step).astype(jnp.int32)
        piece_c = lax.dynamic_slice_in_dim(coords, start, blocks_per_step, 0).astype(jnp.float32)
        piece_w = lax.dynamic_slice_in_dim(weighted, start, blocks_per_step, 0).astype(jnp.float32)
        piece_t = lax.dynamic_slice_in_dim(tile_of[:, 0], start, blocks_per_step, 0)
        return piece_c[:, 0, :] * tile_rows, piece_c[:, 1, :] * tile_cols, piece_w, piece_t

    def forward_step(total, index):
        row_pos, col_pos, piece_w, piece_t = pieces(index)
        left = rounded(kernel_rows(row_pos, tile_rows, lengthscale) * piece_w[:, :, None, :])
        right = rounded(kernel_rows(col_pos, tile_cols, lengthscale))
        contrib = jnp.einsum("bkin,bkjn->bkij", left, right)
        onehot = (piece_t[:, None] == tile_ids[None, :]).astype(jnp.float32)
        return total + jnp.einsum("bt,bkij->tkij", onehot, contrib), None

    start_total = jnp.zeros((tiles, VARS + 1, tile_rows, tile_cols), jnp.float32)
    tiled, _ = lax.scan(forward_step, start_total, jnp.arange(steps_count))
    grid = tiled.reshape(N_LAT, N_LON, VARS + 1, tile_rows, tile_cols)
    grid = grid.transpose(2, 0, 3, 1, 4).reshape(VARS + 1, NLAT, NLON)
    encoded = jnp.einsum("kij,kc->ijc", grid, w_in, precision=lax.Precision.HIGHEST).astype(jnp.bfloat16)
    padded = pad_grid(encoded)
    cells = NLAT * NLON
    pre = jnp.zeros((cells, CH), jnp.float32)
    for p in range(3):
        for q in range(3):
            window = padded[p:p + NLAT, q:q + NLON].reshape(cells, CH)
            pre = pre + jnp.dot(window, w_conv[p, q], preferred_element_type=jnp.float32)
    pre = pre.reshape(NLAT, NLON, CH)
    slope = 0.5 * (1.0 + lax.erf(pre * 0.7071067811865476)) + pre * jnp.exp(-0.5 * pre * pre) * 0.3989422804014327
    grad_pre = (grad_out.astype(jnp.float32) * slope).astype(jnp.bfloat16)
    padded_grad = pad_grid(grad_pre)
    flat_grad = grad_pre.reshape(cells, CH)
    terms = []
    back = grad_out.astype(jnp.float32).reshape(cells, CH)
    for p in range(3):
        for q in range(3):
            window = padded[p:p + NLAT, q:q + NLON].reshape(cells, CH)
            terms.append(jnp.dot(window.T, flat_grad, preferred_element_type=jnp.float32))
            shifted = padded_grad[2 - p:2 - p + NLAT, 2 - q:2 - q + NLON].reshape(cells, CH)
            back = back + jnp.dot(shifted, w_conv[p, q].T, preferred_element_type=jnp.float32)
    grad_conv = jnp.stack(terms).reshape(3, 3, CH, CH)
    back = back.reshape(NLAT, NLON, CH)
    grad_in = jnp.einsum("kij,ijc->kc", grid, back, precision=lax.Precision.HIGHEST)
    grad_grid = jnp.einsum("ijc,kc->kij", back, w_in[:VARS], precision=lax.Precision.HIGHEST).astype(jnp.bfloat16)
    grad_tiles = grad_grid.reshape(VARS, N_LAT, tile_rows, N_LON, tile_cols)
    grad_tiles = grad_tiles.transpose(1, 3, 0, 2, 4).reshape(tiles, VARS, tile_rows, tile_cols)

    def backward_step(carry, index):
        row_pos, col_pos, piece_w, piece_t = pieces(index)
        left = kernel_rows(row_pos, tile_rows, lengthscale[:VARS])
        right = rounded(kernel_rows(col_pos, tile_cols, lengthscale[:VARS]))
        own = grad_tiles[piece_t].astype(jnp.float32)
        middle = jnp.einsum("bkij,bkjn->bkin", own, right)
        term = jnp.sum(left * middle, axis=2) * piece_w[:, VARS:VARS + 1, :]
        return carry, term

    _, outs = lax.scan(backward_step, jnp.zeros((), jnp.float32), jnp.arange(steps_count))
    grad_values = outs.reshape(total_blocks, VARS, coords.shape[2])
    return grad_conv, grad_in, grad_values
```

```python
import jax
import jax.numpy as jnp
from jax import lax
from jax.experimental import pallas as pl
from jax.experimental.pallas import tpu as pltpu
from jax.sharding import PartitionSpec as P


def with_halo(cells, sides, width):
    for axis, dim in sides:
        count = lax.axis_size(axis)
        head = lax.slice_in_dim(cells, 0, width, axis=dim)
        tail = lax.slice_in_dim(cells, cells.shape[dim] - width, cells.shape[dim], axis=dim)
        cells = jnp.concatenate(
            [
                lax.ppermute(tail, axis, [(i, (i + 1) % count) for i in range(count)]),
                cells,
                lax.ppermute(head, axis, [((i + 1) % count, i) for i in range(count)]),
            ],
            axis=dim,
        )
    return cells


def squares(position, count):
    width = position.shape[1]
    centers = lax.broadcasted_iota(jnp.int32, (count, width), 0).astype(jnp.float32) + 0.5
    diff = centers - position
    return diff * diff


def rates(lengthscale):
    return -1.4426950408889634 / (2.0 * lengthscale * lengthscale)


def gather_kernel(tile_ref, rate_ref, coords_ref, values_ref, live_ref, out_ref, total):
    variables = values_ref.shape[1]
    tile_rows, tile_cols = total.shape[2:]
    rows_dev = out_ref.shape[2]
    total[...] = jnp.zeros_like(total)

    def one(n, carry):
        t = tile_ref[n]
        place = coords_ref[n].astype(jnp.float32)
        mask = live_ref[pl.ds(n, 1), :].astype(jnp.float32)
        weighted = values_ref[n].astype(jnp.float32) * mask
        row_sq = squares(place[0:1] * tile_rows, tile_rows)
        col_sq = squares(place[1:2] * tile_cols, tile_cols)
        for k in range(variables + 1):
            w = weighted[k : k + 1] if k < variables else mask
            left = (jnp.exp2(row_sq * rate_ref[k]) * w).astype(jnp.bfloat16)
            right = jnp.exp2(col_sq * rate_ref[k]).astype(jnp.bfloat16)
            total[t, k] += lax.dot_general(
                left, right, (((1,), (1,)), ((), ())), preferred_element_type=jnp.float32
            )
        return carry

    lax.fori_loop(0, coords_ref.shape[0], one, 0)

    def flush(t, carry):
        for o in range(tile_rows // rows_dev):
            for k in range(variables + 1):
                out_ref[t * (tile_rows // rows_dev) + o, k] = total[
                    t, k, o * rows_dev : (o + 1) * rows_dev
                ].astype(jnp.bfloat16)
        return carry

    lax.fori_loop(0, total.shape[0], flush, 0)


def value_kernel(tile_ref, rate_ref, coords_ref, live_ref, grad_ref, out_ref):
    variables = out_ref.shape[1]
    tile_rows, tile_cols = grad_ref.shape[2:]

    def one(n, carry):
        t = tile_ref[n]
        place = coords_ref[n].astype(jnp.float32)
        mask = live_ref[pl.ds(n, 1), :].astype(jnp.float32)
        row_sq = squares(place[0:1] * tile_rows, tile_rows)
        col_sq = squares(place[1:2] * tile_cols, tile_cols)
        for k in range(variables):
            left = jnp.exp2(row_sq * rate_ref[k])
            right = jnp.exp2(col_sq * rate_ref[k]).astype(jnp.bfloat16)
            middle = jnp.dot(grad_ref[t, k], right, preferred_element_type=jnp.float32)
            out_ref[n, k : k + 1] = jnp.sum(left * middle, axis=0, keepdims=True) * mask
        return carry

    lax.fori_loop(0, coords_ref.shape[0], one, 0)


def with_rims(field):
    padded = with_halo(field, ((("lat", "obs"), 0), ("lon", 1)), 1)
    place = lax.axis_index("lat") * lax.axis_size("obs") + lax.axis_index("obs")
    last_place = lax.axis_size("lat") * lax.axis_size("obs") - 1
    row_ids = jnp.arange(padded.shape[0])
    keep = jnp.where(
        row_ids == 0, place > 0, jnp.where(row_ids == padded.shape[0] - 1, place < last_place, True)
    )
    return padded * keep[:, None, None].astype(padded.dtype)


def body(coords, values, live, tile_of, lengthscale, w_in, w_conv, grad_out):
    lat_count = lax.axis_size("lat")
    lon_count = lax.axis_size("lon")
    obs_count = lax.axis_size("obs")
    tiles = lat_count * lon_count
    blocks = coords.shape[0]
    width = coords.shape[2]
    variables = values.shape[1]
    rows_dev, tile_cols, channels = grad_out.shape
    tile_rows = rows_dev * obs_count
    everyone = ("lat", "lon", "obs")
    rate = rates(lengthscale)
    target = tile_of[:, 0]
    smem = pl.BlockSpec(memory_space=pltpu.SMEM)
    vmem = pl.BlockSpec(memory_space=pltpu.VMEM)
    exps = blocks * width * (tile_rows + tile_cols)
    partial_value = pl.pallas_call(
        gather_kernel,
        out_shape=jax.ShapeDtypeStruct(
            (tiles * obs_count, variables + 1, rows_dev, tile_cols), jnp.bfloat16
        ),
        in_specs=[smem, smem, vmem, vmem, vmem],
        out_specs=vmem,
        scratch_shapes=[
            pltpu.VMEM((tiles, variables + 1, tile_rows, tile_cols), jnp.float32)
        ],
        compiler_params=pltpu.CompilerParams(vmem_limit_bytes=40 * 1024 * 1024),
    )(target, rate, coords, values, live)
    parts = lax.all_to_all(partial_value, everyone, split_axis=0, concat_axis=0, tiled=True)
    grid = jnp.sum(parts.astype(jnp.float32), axis=0)
    encoded = jnp.einsum("kij,kc->ijc", grid, w_in, precision=lax.Precision.HIGHEST).astype(
        jnp.bfloat16
    )
    padded = with_rims(encoded)
    pre = jnp.zeros((rows_dev, tile_cols, channels), jnp.float32)
    for p in range(3):
        for q in range(3):
            pre = pre + jnp.einsum(
                "ijc,cd->ijd",
                padded[p : p + rows_dev, q : q + tile_cols],
                w_conv[p, q],
                preferred_element_type=jnp.float32,
            )
    slope = (
        0.5 * (1.0 + lax.erf(pre * 0.7071067811865476))
        + pre * jnp.exp(-0.5 * pre * pre) * 0.3989422804014327
    )
    grad_pre = (grad_out.astype(jnp.float32) * slope).astype(jnp.bfloat16)
    padded_grad = with_rims(grad_pre)
    terms = []
    back = grad_out.astype(jnp.float32)
    for p in range(3):
        for q in range(3):
            terms.append(
                jnp.einsum(
                    "ijc,ijd->cd",
                    padded[p : p + rows_dev, q : q + tile_cols],
                    grad_pre,
                    preferred_element_type=jnp.float32,
                )
            )
            back = back + jnp.einsum(
                "ijd,cd->ijc",
                padded_grad[2 - p : 2 - p + rows_dev, 2 - q : 2 - q + tile_cols],
                w_conv[p, q],
                preferred_element_type=jnp.float32,
            )
    conv_part = jnp.stack(terms).reshape(3, 3, channels, channels)
    input_part = jnp.einsum("kij,ijc->kc", grid, back, precision=lax.Precision.HIGHEST)
    grad_grid = jnp.einsum(
        "ijc,kc->kij", back, w_in[:variables], precision=lax.Precision.HIGHEST
    ).astype(jnp.bfloat16)
    devices = lat_count * lon_count * obs_count
    pieces = conv_part.reshape(devices, -1, channels).astype(jnp.bfloat16)
    pieces = lax.all_to_all(pieces, everyone, split_axis=0, concat_axis=0, tiled=True)
    piece = jnp.sum(pieces.astype(jnp.float32), axis=0).astype(jnp.bfloat16)
    input_parts = lax.all_gather(input_part, everyone, axis=0, tiled=False)
    grad_in = jnp.sum(input_parts, axis=0)
    tile_grad = lax.all_gather(grad_grid, everyone, axis=0, tiled=False)
    tile_grad = tile_grad.reshape(tiles, obs_count, variables, rows_dev, tile_cols)
    tile_grad = tile_grad.transpose(0, 2, 1, 3, 4).reshape(tiles, variables, tile_rows, tile_cols)
    whole_conv = lax.all_gather(piece, everyone, axis=0, tiled=True)
    grad_conv = whole_conv.astype(jnp.float32).reshape(3, 3, channels, channels)
    grad_values = pl.pallas_call(
        value_kernel,
        out_shape=jax.ShapeDtypeStruct((blocks, variables, width), jnp.float32),
        in_specs=[smem, smem, vmem, vmem, vmem],
        out_specs=vmem,
        compiler_params=pltpu.CompilerParams(vmem_limit_bytes=40 * 1024 * 1024),
        cost_estimate=pl.CostEstimate(
            flops=40000000000, bytes_accessed=4000000, transcendentals=exps * variables
        ),
    )(target, rate, coords, live, tile_grad)
    return (grad_conv, grad_in, grad_values)


def solution(mesh):
    placed = (
        P(("lat", "lon", "obs"), None, None),
        P(("lat", "lon", "obs"), None, None),
        P(("lat", "lon", "obs"), None),
        P(("lat", "lon", "obs"), None),
        P(),
        P(),
        P(),
        P(("lat", "obs"), "lon", None),
    )
    return jax.shard_map(
        body,
        mesh=mesh,
        in_specs=placed,
        out_specs=(P(), P(), P(("lat", "lon", "obs"), None, None)),
        check_vma=False,
    )
```

```python
import jax
import jax.numpy as jnp
from jax import lax
from jax.experimental import pallas as pl
from jax.experimental.pallas import tpu as pltpu
from jax.sharding import PartitionSpec as P


def with_halo(cells, sides, width):
    for axis, dim in sides:
        count = lax.axis_size(axis)
        head = lax.slice_in_dim(cells, 0, width, axis=dim)
        tail = lax.slice_in_dim(cells, cells.shape[dim] - width, cells.shape[dim], axis=dim)
        cells = jnp.concatenate(
            [
                lax.ppermute(tail, axis, [(i, (i + 1) % count) for i in range(count)]),
                cells,
                lax.ppermute(head, axis, [((i + 1) % count, i) for i in range(count)]),
            ],
            axis=dim,
        )
    return cells


def squares(position, count):
    width = position.shape[1]
    centers = lax.broadcasted_iota(jnp.int32, (count, width), 0).astype(jnp.float32) + 0.5
    diff = centers - position
    return diff * diff


def rates(lengthscale):
    return -1.4426950408889634 / (2.0 * lengthscale * lengthscale)


def gather_kernel(tile_ref, rate_ref, coords_ref, values_ref, live_ref, out_ref, total):
    variables = values_ref.shape[1]
    tile_rows, tile_cols = total.shape[2:]
    rows_dev = out_ref.shape[2]
    total[...] = jnp.zeros_like(total)

    def one(n, carry):
        t = tile_ref[n]
        place = coords_ref[n].astype(jnp.float32)
        mask = live_ref[pl.ds(n, 1), :].astype(jnp.float32)
        weighted = values_ref[n].astype(jnp.float32) * mask
        row_sq = squares(place[0:1] * tile_rows, tile_rows)
        col_sq = squares(place[1:2] * tile_cols, tile_cols)
        for k in range(variables + 1):
            w = weighted[k : k + 1] if k < variables else mask
            left = (jnp.exp2(row_sq * rate_ref[k]) * w).astype(jnp.bfloat16)
            right = jnp.exp2(col_sq * rate_ref[k]).astype(jnp.bfloat16)
            total[t, k] += lax.dot_general(
                left, right, (((1,), (1,)), ((), ())), preferred_element_type=jnp.float32
            )
        return carry

    lax.fori_loop(0, coords_ref.shape[0], one, 0)

    def flush(t, carry):
        for o in range(tile_rows // rows_dev):
            for k in range(variables + 1):
                out_ref[t * (tile_rows // rows_dev) + o, k] = total[
                    t, k, o * rows_dev : (o + 1) * rows_dev
                ].astype(jnp.bfloat16)
        return carry

    lax.fori_loop(0, total.shape[0], flush, 0)


def signal_peers(axes):
    barrier = pltpu.get_barrier_semaphore()
    greeted = 0
    for axis in axes:
        count = lax.axis_size(axis)
        me = lax.axis_index(axis)
        for step in range(1, count):
            pl.semaphore_signal(
                barrier,
                inc=1,
                device_id={axis: lax.rem(me + step, count)},
                device_id_type=pl.DeviceIdType.MESH,
            )
            greeted += 1
    pl.semaphore_wait(barrier, greeted)


def start_copies(axis, source_of, target, sems):
    count = lax.axis_size(axis)
    me = lax.axis_index(axis)
    copies = []
    for step in range(1, count):
        peer = lax.rem(me + step, count)
        copy = pltpu.make_async_remote_copy(
            src_ref=source_of(peer),
            dst_ref=target,
            send_sem=sems.at[0, step],
            recv_sem=sems.at[1, step],
            device_id={axis: peer},
            device_id_type=pl.DeviceIdType.MESH,
        )
        copy.start()
        copies.append(copy)
    return copies


def wait_all(copies):
    for copy in copies:
        copy.wait()


def value_kernel(
    slot_ref,
    rate_ref,
    coords_ref,
    live_ref,
    grad_ref,
    input_ref,
    conv_ref,
    out_ref,
    input_out,
    conv_out,
    cells,
    tile_grad,
    own_in1,
    own_in2,
    in1,
    in2,
    in3,
    got1,
    sum1,
    got2,
    sum2,
    got3,
    whole,
    sems,
):
    blocks, variables = out_ref.shape[:2]
    lat_count, lon_count, obs_count = (lax.axis_size(a) for a in ("lat", "lon", "obs"))
    lat, lon, obs = (lax.axis_index(a) for a in ("lat", "lon", "obs"))
    tile_rows, tile_cols = tile_grad.shape[2:]
    rows_dev = tile_rows // obs_count
    signal_peers(("lat", "lon", "obs"))

    reduce1 = start_copies("lon", lambda peer: conv_ref.at[peer], got1.at[lon], sems.at[0])
    home = lon * lat_count + lat
    cells[home, obs] = grad_ref[...]
    in1[obs] = input_ref[...]
    mine = cells.at[home, obs]
    gather1 = start_copies("obs", lambda peer: mine, mine, sems.at[1])
    gather1 += start_copies("obs", lambda peer: input_ref, in1.at[obs], sems.at[2])
    wait_all(gather1)
    total = jnp.sum(in1[...], axis=0)
    own_in1[...] = total
    in2[lat] = total
    gather2 = start_copies("lat", lambda peer: cells.at[home], cells.at[home], sems.at[3])
    gather2 += start_copies("lat", lambda peer: own_in1, in2.at[lat], sems.at[4])

    wait_all(reduce1)

    def add1(i, carry):
        value = conv_ref[lon, i]
        for step in range(1, lon_count):
            value = value + got1[lax.rem(lon + step, lon_count), i]
        sum1[i // obs_count, i % obs_count] = value.astype(jnp.bfloat16)
        return carry

    lax.fori_loop(0, lat_count * obs_count, add1, 0)
    reduce2 = start_copies("lat", lambda peer: sum1.at[peer], got2.at[lat], sems.at[5])
    wait_all(gather2)
    total = jnp.sum(in2[...], axis=0)
    own_in2[...] = total
    in3[lon] = total
    group = pl.ds(lon * lat_count, lat_count)
    gather3 = start_copies("lon", lambda peer: cells.at[group], cells.at[group], sems.at[6])
    gather3 += start_copies("lon", lambda peer: own_in2, in3.at[lon], sems.at[7])
    wait_all(gather3)
    input_out[...] = jnp.sum(in3[...], axis=0)

    def spread(t, carry):
        for o in range(obs_count):
            piece = cells[t, o].astype(jnp.float32)
            for k in range(variables):
                tile_grad[t, k, o * rows_dev : (o + 1) * rows_dev] = piece[
                    k * rows_dev : (k + 1) * rows_dev
                ]
        return carry

    lax.fori_loop(0, tile_grad.shape[0], spread, 0)

    def one(n, carry):
        t = slot_ref[n]
        place = coords_ref[n].astype(jnp.float32)
        mask = live_ref[pl.ds(n, 1), :].astype(jnp.float32)
        row_sq = squares(place[0:1] * tile_rows, tile_rows)
        col_sq = squares(place[1:2] * tile_cols, tile_cols)
        for k in range(variables):
            left = jnp.exp2(row_sq * rate_ref[k])
            right = jnp.exp2(col_sq * rate_ref[k]).astype(jnp.bfloat16)
            middle = jnp.dot(
                tile_grad[t, k].astype(jnp.bfloat16), right, preferred_element_type=jnp.float32
            )
            out_ref[n, k : k + 1] = jnp.sum(left * middle, axis=0, keepdims=True) * mask
        return carry

    def some(first, last):
        lax.fori_loop(first * blocks // 64, last * blocks // 64, one, 0)

    some(0, 8)
    wait_all(reduce2)

    def add2(i, carry):
        value = sum1[lat, i].astype(jnp.float32)
        for step in range(1, lat_count):
            value = value + got2[lax.rem(lat + step, lat_count), i].astype(jnp.float32)
        sum2[i] = value
        return carry

    lax.fori_loop(0, obs_count, add2, 0)
    reduce3 = start_copies("obs", lambda peer: sum2.at[peer], got3.at[obs], sems.at[8])
    some(8, 24)
    wait_all(reduce3)
    value = sum2[obs]
    for step in range(1, obs_count):
        value = value + got3[lax.rem(obs + step, obs_count)]
    whole[lon, lat, obs] = value.astype(jnp.bfloat16)
    mine1 = whole.at[lon, lat, obs]
    spread1 = start_copies("obs", lambda peer: mine1, mine1, sems.at[9])
    some(24, 34)
    wait_all(spread1)
    mine2 = whole.at[lon, lat]
    spread2 = start_copies("lat", lambda peer: mine2, mine2, sems.at[10])
    some(34, 54)
    wait_all(spread2)
    mine3 = whole.at[lon]
    spread3 = start_copies("lon", lambda peer: mine3, mine3, sems.at[11])
    some(54, 64)
    wait_all(spread3)

    def give(i, carry):
        a, b = i // lat_count, i % lat_count
        for o in range(obs_count):
            conv_out[a, b, o] = whole[a, b, o]
        return carry

    lax.fori_loop(0, lon_count * lat_count, give, 0)


def with_rims(field):
    padded = with_halo(field, ((("lat", "obs"), 0), ("lon", 1)), 1)
    place = lax.axis_index("lat") * lax.axis_size("obs") + lax.axis_index("obs")
    last_place = lax.axis_size("lat") * lax.axis_size("obs") - 1
    row_ids = jnp.arange(padded.shape[0])
    keep = jnp.where(
        row_ids == 0, place > 0, jnp.where(row_ids == padded.shape[0] - 1, place < last_place, True)
    )
    return padded * keep[:, None, None].astype(padded.dtype)


def body(coords, values, live, tile_of, lengthscale, w_in, w_conv, grad_out):
    lat_count = lax.axis_size("lat")
    lon_count = lax.axis_size("lon")
    obs_count = lax.axis_size("obs")
    tiles = lat_count * lon_count
    blocks = coords.shape[0]
    width = coords.shape[2]
    variables = values.shape[1]
    rows_dev, tile_cols, channels = grad_out.shape
    tile_rows = rows_dev * obs_count
    everyone = ("lat", "lon", "obs")
    rate = rates(lengthscale)
    target = tile_of[:, 0]
    smem = pl.BlockSpec(memory_space=pltpu.SMEM)
    vmem = pl.BlockSpec(memory_space=pltpu.VMEM)
    exps = blocks * width * (tile_rows + tile_cols)
    partial_value = pl.pallas_call(
        gather_kernel,
        out_shape=jax.ShapeDtypeStruct(
            (tiles * obs_count, variables + 1, rows_dev, tile_cols), jnp.bfloat16
        ),
        in_specs=[smem, smem, vmem, vmem, vmem],
        out_specs=vmem,
        scratch_shapes=[
            pltpu.VMEM((tiles, variables + 1, tile_rows, tile_cols), jnp.float32)
        ],
        compiler_params=pltpu.CompilerParams(vmem_limit_bytes=40 * 1024 * 1024),
    )(target, rate, coords, values, live)
    parts = lax.all_to_all(partial_value, everyone, split_axis=0, concat_axis=0, tiled=True)
    grid = jnp.sum(parts.astype(jnp.float32), axis=0)
    encoded = jnp.einsum("kij,kc->ijc", grid, w_in, precision=lax.Precision.HIGHEST).astype(
        jnp.bfloat16
    )
    padded = with_rims(encoded)
    pre = jnp.zeros((rows_dev, tile_cols, channels), jnp.float32)
    for p in range(3):
        for q in range(3):
            pre = pre + jnp.einsum(
                "ijc,cd->ijd",
                padded[p : p + rows_dev, q : q + tile_cols],
                w_conv[p, q],
                preferred_element_type=jnp.float32,
            )
    slope = (
        0.5 * (1.0 + lax.erf(pre * 0.7071067811865476))
        + pre * jnp.exp(-0.5 * pre * pre) * 0.3989422804014327
    )
    grad_pre = (grad_out.astype(jnp.float32) * slope).astype(jnp.bfloat16)
    padded_grad = with_rims(grad_pre)
    terms = []
    back = grad_out.astype(jnp.float32)
    for p in range(3):
        for q in range(3):
            terms.append(
                jnp.einsum(
                    "ijc,ijd->cd",
                    padded[p : p + rows_dev, q : q + tile_cols],
                    grad_pre,
                    preferred_element_type=jnp.float32,
                )
            )
            back = back + jnp.einsum(
                "ijd,cd->ijc",
                padded_grad[2 - p : 2 - p + rows_dev, 2 - q : 2 - q + tile_cols],
                w_conv[p, q],
                preferred_element_type=jnp.float32,
            )
    conv_part = jnp.stack(terms).reshape(3, 3, channels, channels)
    input_part = jnp.einsum("kij,ijc->kc", grid, back, precision=lax.Precision.HIGHEST)
    grad_grid = jnp.einsum(
        "ijc,kc->kij", back, w_in[:variables], precision=lax.Precision.HIGHEST
    ).astype(jnp.bfloat16)
    chunk = conv_part.size // (lat_count * lon_count * obs_count * channels)
    most = max(lat_count, lon_count, obs_count)
    held = ((variables + 1 + 7) // 8) * 8
    input_part = jnp.pad(input_part, ((0, held - variables - 1), (0, 0)))
    f32, bf16 = jnp.float32, jnp.bfloat16
    slots = (target % lon_count) * lat_count + target // lon_count
    grad_values, grad_in, whole_conv = pl.pallas_call(
        value_kernel,
        out_shape=(
            jax.ShapeDtypeStruct((blocks, variables, width), f32),
            jax.ShapeDtypeStruct((held, channels), f32),
            jax.ShapeDtypeStruct((lon_count, lat_count, obs_count, chunk, channels), bf16),
        ),
        in_specs=[smem, smem, vmem, vmem, vmem, vmem, vmem],
        out_specs=(vmem, vmem, vmem),
        scratch_shapes=[
            pltpu.VMEM((tiles, obs_count, variables * rows_dev, tile_cols), bf16),
            pltpu.VMEM((tiles, variables, tile_rows, tile_cols), f32),
            pltpu.VMEM((held, channels), f32),
            pltpu.VMEM((held, channels), f32),
            pltpu.VMEM((obs_count, held, channels), f32),
            pltpu.VMEM((lat_count, held, channels), f32),
            pltpu.VMEM((lon_count, held, channels), f32),
            pltpu.VMEM((lon_count, lat_count * obs_count, chunk, channels), f32),
            pltpu.VMEM((lat_count, obs_count, chunk, channels), bf16),
            pltpu.VMEM((lat_count, obs_count, chunk, channels), bf16),
            pltpu.VMEM((obs_count, chunk, channels), f32),
            pltpu.VMEM((obs_count, chunk, channels), f32),
            pltpu.VMEM((lon_count, lat_count, obs_count, chunk, channels), bf16),
            pltpu.SemaphoreType.DMA((12, 2, most)),
        ],
        compiler_params=pltpu.CompilerParams(
            vmem_limit_bytes=48 * 1024 * 1024, collective_id=1, has_side_effects=True
        ),
        cost_estimate=pl.CostEstimate(
            flops=4000000000, bytes_accessed=8000000, transcendentals=exps * variables
        ),
    )(
        slots,
        rate,
        coords,
        live,
        grad_grid.reshape(variables * rows_dev, tile_cols),
        input_part,
        conv_part.reshape(lon_count, lat_count * obs_count, chunk, channels),
    )
    grad_in = grad_in[: variables + 1]
    grad_conv = whole_conv.astype(f32).reshape(3, 3, channels, channels)
    return (grad_conv, grad_in, grad_values)


def solution(mesh):
    placed = (
        P(("lat", "lon", "obs"), None, None),
        P(("lat", "lon", "obs"), None, None),
        P(("lat", "lon", "obs"), None),
        P(("lat", "lon", "obs"), None),
        P(),
        P(),
        P(),
        P(("lat", "obs"), "lon", None),
    )
    return jax.shard_map(
        body,
        mesh=mesh,
        in_specs=placed,
        out_specs=(P(), P(), P(("lat", "lon", "obs"), None, None)),
        check_vma=False,
    )
```

```python
import jax
import jax.numpy as jnp
from jax import lax
from jax.experimental import pallas as pl
from jax.experimental.pallas import tpu as pltpu
from jax.sharding import PartitionSpec as P


def with_halo(cells, sides, width):
    for axis, dim in sides:
        count = lax.axis_size(axis)
        head = lax.slice_in_dim(cells, 0, width, axis=dim)
        tail = lax.slice_in_dim(cells, cells.shape[dim] - width, cells.shape[dim], axis=dim)
        cells = jnp.concatenate(
            [
                lax.ppermute(tail, axis, [(i, (i + 1) % count) for i in range(count)]),
                cells,
                lax.ppermute(head, axis, [((i + 1) % count, i) for i in range(count)]),
            ],
            axis=dim,
        )
    return cells


def squares(position, count):
    width = position.shape[1]
    centers = lax.broadcasted_iota(jnp.int32, (count, width), 0).astype(jnp.float32) + 0.5
    diff = centers - position
    return diff * diff


def rates(lengthscale):
    return -1.4426950408889634 / (2.0 * lengthscale * lengthscale)


def gather_kernel(tile_ref, rate_ref, coords_ref, values_ref, live_ref, out_ref, total):
    variables = values_ref.shape[1]
    tile_rows, tile_cols = total.shape[2:]
    rows_dev = out_ref.shape[3]
    total[...] = jnp.zeros_like(total)

    def one(n, carry):
        t = tile_ref[n]
        place = coords_ref[n].astype(jnp.float32)
        mask = live_ref[pl.ds(n, 1), :].astype(jnp.float32)
        weighted = values_ref[n].astype(jnp.float32) * mask
        row_sq = squares(place[0:1] * tile_rows, tile_rows)
        col_sq = squares(place[1:2] * tile_cols, tile_cols)
        for k in range(variables + 1):
            w = weighted[k : k + 1] if k < variables else mask
            left = (jnp.exp2(row_sq * rate_ref[k]) * w).astype(jnp.bfloat16)
            right = jnp.exp2(col_sq * rate_ref[k]).astype(jnp.bfloat16)
            total[t, k] += lax.dot_general(
                left, right, (((1,), (1,)), ((), ())), preferred_element_type=jnp.float32
            )
        return carry

    lax.fori_loop(0, coords_ref.shape[0], one, 0)

    def flush(t, carry):
        for o in range(tile_rows // rows_dev):
            for k in range(variables + 1):
                out_ref[t, o, k] = total[t, k, o * rows_dev : (o + 1) * rows_dev]
        return carry

    lax.fori_loop(0, total.shape[0], flush, 0)


def signal_peers(axes, greeted=0):
    barrier = pltpu.get_barrier_semaphore()
    for axis in axes:
        count = lax.axis_size(axis)
        me = lax.axis_index(axis)
        for step in range(1, count):
            pl.semaphore_signal(
                barrier,
                inc=1,
                device_id={axis: lax.rem(me + step, count)},
                device_id_type=pl.DeviceIdType.MESH,
            )
            greeted += 1
    pl.semaphore_wait(barrier, greeted)


def start_copies(axis, source_of, target, sems):
    count = lax.axis_size(axis)
    me = lax.axis_index(axis)
    copies = []
    for step in range(1, count):
        peer = lax.rem(me + step, count)
        copy = pltpu.make_async_remote_copy(
            src_ref=source_of(peer),
            dst_ref=target,
            send_sem=sems.at[0, step],
            recv_sem=sems.at[1, step],
            device_id={axis: peer},
            device_id_type=pl.DeviceIdType.MESH,
        )
        copy.start()
        copies.append(copy)
    return copies


def wait_all(copies):
    for copy in copies:
        copy.wait()


def reduce_kernel(part_ref, out_ref, got1, sum1, got2, sum2, got3, rows, sides, sems):
    lat_count, lon_count, obs_count = (lax.axis_size(a) for a in ("lat", "lon", "obs"))
    lat, lon, obs = (lax.axis_index(a) for a in ("lat", "lon", "obs"))
    rows_dev = rows.shape[0] - 2
    levels = sum1.shape[2] // rows_dev
    mesh_ids = pl.DeviceIdType.MESH
    places = lat_count * obs_count
    place = lat * obs_count + obs
    after = lax.rem(place + 1, places)
    before = lax.rem(place + places - 1, places)
    down = {"lat": after // obs_count, "obs": lax.rem(after, obs_count)}
    up = {"lat": before // obs_count, "obs": lax.rem(before, obs_count)}
    east = {"lon": lax.rem(lon + 1, lon_count)}
    west = {"lon": lax.rem(lon + lon_count - 1, lon_count)}
    rows[...] = jnp.zeros_like(rows)
    barrier = pltpu.get_barrier_semaphore()
    for device in (up, down):
        pl.semaphore_signal(barrier, inc=1, device_id=device, device_id_type=mesh_ids)
    signal_peers(("lat", "lon", "obs"), 2)

    wait_all(start_copies("lon", lambda peer: part_ref.at[peer], got1.at[lon], sems.at[0]))

    def add1(i, carry):
        value = part_ref[lon, i]
        for step in range(1, lon_count):
            value = value + got1[lax.rem(lon + step, lon_count), i]
        sum1[i // obs_count, i % obs_count] = value.astype(jnp.bfloat16)
        return carry

    lax.fori_loop(0, lat_count * obs_count, add1, 0)
    wait_all(start_copies("lat", lambda peer: sum1.at[peer], got2.at[lat], sems.at[1]))

    def add2(i, carry):
        value = sum1[lat, i].astype(jnp.float32)
        for step in range(1, lat_count):
            value = value + got2[lax.rem(lat + step, lat_count), i].astype(jnp.float32)
        sum2[i] = value
        return carry

    lax.fori_loop(0, obs_count, add2, 0)
    wait_all(start_copies("obs", lambda peer: sum2.at[peer], got3.at[obs], sems.at[2]))
    value = sum2[obs]
    for step in range(1, obs_count):
        value = value + got3[lax.rem(obs + step, obs_count)]
    for k in range(levels):
        for r in range(rows_dev):
            rows[r + 1, k : k + 1] = value[k * rows_dev + r : k * rows_dev + r + 1]

    def send(source, target, number, device):
        copy = pltpu.make_async_remote_copy(
            src_ref=source,
            dst_ref=target,
            send_sem=sems.at[3, 0, number],
            recv_sem=sems.at[3, 1, number],
            device_id=device,
            device_id_type=mesh_ids,
        )
        copy.start()
        return copy

    wait_all(
        [
            send(rows.at[1], rows.at[rows_dev + 1], 0, up),
            send(rows.at[rows_dev], rows.at[0], 1, down),
        ]
    )
    rows[0] = rows[0] * (place > 0).astype(jnp.float32)
    rows[rows_dev + 1] = rows[rows_dev + 1] * (place < places - 1).astype(jnp.float32)
    wait_all([send(rows, sides.at[1], 2, west), send(rows, sides.at[0], 3, east)])
    out_ref[0] = sides[0]
    out_ref[1] = rows[...]
    out_ref[2] = sides[1]


def value_kernel(
    slot_ref,
    rate_ref,
    coords_ref,
    live_ref,
    grad_ref,
    input_ref,
    conv_ref,
    out_ref,
    input_out,
    conv_out,
    cells,
    tile_grad,
    own_in1,
    own_in2,
    in1,
    in2,
    in3,
    got1,
    sum1,
    got2,
    sum2,
    got3,
    whole,
    sems,
):
    blocks, variables = out_ref.shape[:2]
    lat_count, lon_count, obs_count = (lax.axis_size(a) for a in ("lat", "lon", "obs"))
    lat, lon, obs = (lax.axis_index(a) for a in ("lat", "lon", "obs"))
    tile_rows, tile_cols = tile_grad.shape[2:]
    rows_dev = tile_rows // obs_count
    signal_peers(("lat", "lon", "obs"))

    reduce1 = start_copies("lon", lambda peer: conv_ref.at[peer], got1.at[lon], sems.at[0])
    home = lon * lat_count + lat
    cells[home, obs] = grad_ref[...]
    in1[obs] = input_ref[...]
    mine = cells.at[home, obs]
    gather1 = start_copies("obs", lambda peer: mine, mine, sems.at[1])
    gather1 += start_copies("obs", lambda peer: input_ref, in1.at[obs], sems.at[2])
    wait_all(gather1)
    total = jnp.sum(in1[...], axis=0)
    own_in1[...] = total
    in2[lat] = total
    gather2 = start_copies("lat", lambda peer: cells.at[home], cells.at[home], sems.at[3])
    gather2 += start_copies("lat", lambda peer: own_in1, in2.at[lat], sems.at[4])

    wait_all(reduce1)

    def add1(i, carry):
        value = conv_ref[lon, i]
        for step in range(1, lon_count):
            value = value + got1[lax.rem(lon + step, lon_count), i]
        sum1[i // obs_count, i % obs_count] = value.astype(jnp.bfloat16)
        return carry

    lax.fori_loop(0, lat_count * obs_count, add1, 0)
    reduce2 = start_copies("lat", lambda peer: sum1.at[peer], got2.at[lat], sems.at[5])
    wait_all(gather2)
    total = jnp.sum(in2[...], axis=0)
    own_in2[...] = total
    in3[lon] = total
    group = pl.ds(lon * lat_count, lat_count)
    gather3 = start_copies("lon", lambda peer: cells.at[group], cells.at[group], sems.at[6])
    gather3 += start_copies("lon", lambda peer: own_in2, in3.at[lon], sems.at[7])
    wait_all(gather3)
    input_out[...] = jnp.sum(in3[...], axis=0)

    def spread(t, carry):
        for o in range(obs_count):
            piece = cells[t, o].astype(jnp.float32)
            for k in range(variables):
                tile_grad[t, k, o * rows_dev : (o + 1) * rows_dev] = piece[
                    k * rows_dev : (k + 1) * rows_dev
                ]
        return carry

    lax.fori_loop(0, tile_grad.shape[0], spread, 0)

    def one(n, carry):
        t = slot_ref[n]
        place = coords_ref[n].astype(jnp.float32)
        mask = live_ref[pl.ds(n, 1), :].astype(jnp.float32)
        row_sq = squares(place[0:1] * tile_rows, tile_rows)
        col_sq = squares(place[1:2] * tile_cols, tile_cols)
        for k in range(variables):
            left = jnp.exp2(row_sq * rate_ref[k])
            right = jnp.exp2(col_sq * rate_ref[k]).astype(jnp.bfloat16)
            middle = jnp.dot(
                tile_grad[t, k].astype(jnp.bfloat16), right, preferred_element_type=jnp.float32
            )
            out_ref[n, k : k + 1] = jnp.sum(left * middle, axis=0, keepdims=True) * mask
        return carry

    def some(first, last):
        lax.fori_loop(first * blocks // 64, last * blocks // 64, one, 0)

    some(0, 8)
    wait_all(reduce2)

    def add2(i, carry):
        value = sum1[lat, i].astype(jnp.float32)
        for step in range(1, lat_count):
            value = value + got2[lax.rem(lat + step, lat_count), i].astype(jnp.float32)
        sum2[i] = value
        return carry

    lax.fori_loop(0, obs_count, add2, 0)
    reduce3 = start_copies("obs", lambda peer: sum2.at[peer], got3.at[obs], sems.at[8])
    some(8, 24)
    wait_all(reduce3)
    value = sum2[obs]
    for step in range(1, obs_count):
        value = value + got3[lax.rem(obs + step, obs_count)]
    whole[lon, lat, obs] = value.astype(jnp.bfloat16)
    mine1 = whole.at[lon, lat, obs]
    spread1 = start_copies("obs", lambda peer: mine1, mine1, sems.at[9])
    some(24, 34)
    wait_all(spread1)
    mine2 = whole.at[lon, lat]
    spread2 = start_copies("lat", lambda peer: mine2, mine2, sems.at[10])
    some(34, 54)
    wait_all(spread2)
    mine3 = whole.at[lon]
    spread3 = start_copies("lon", lambda peer: mine3, mine3, sems.at[11])
    some(54, 64)
    wait_all(spread3)

    def give(i, carry):
        a, b = i // lat_count, i % lat_count
        for o in range(obs_count):
            conv_out[a, b, o] = whole[a, b, o]
        return carry

    lax.fori_loop(0, lon_count * lat_count, give, 0)


def with_rims(field):
    padded = with_halo(field, ((("lat", "obs"), 0), ("lon", 1)), 1)
    place = lax.axis_index("lat") * lax.axis_size("obs") + lax.axis_index("obs")
    last_place = lax.axis_size("lat") * lax.axis_size("obs") - 1
    row_ids = jnp.arange(padded.shape[0])
    keep = jnp.where(
        row_ids == 0, place > 0, jnp.where(row_ids == padded.shape[0] - 1, place < last_place, True)
    )
    return padded * keep[:, None, None].astype(padded.dtype)


def body(coords, values, live, tile_of, lengthscale, w_in, w_conv, grad_out):
    lat_count = lax.axis_size("lat")
    lon_count = lax.axis_size("lon")
    obs_count = lax.axis_size("obs")
    tiles = lat_count * lon_count
    blocks = coords.shape[0]
    width = coords.shape[2]
    variables = values.shape[1]
    rows_dev, tile_cols, channels = grad_out.shape
    tile_rows = rows_dev * obs_count
    everyone = ("lat", "lon", "obs")
    rate = rates(lengthscale)
    target = tile_of[:, 0]
    smem = pl.BlockSpec(memory_space=pltpu.SMEM)
    vmem = pl.BlockSpec(memory_space=pltpu.VMEM)
    exps = blocks * width * (tile_rows + tile_cols)
    f32, bf16 = jnp.float32, jnp.bfloat16
    slots = (target % lon_count) * lat_count + target // lon_count
    partial_value = pl.pallas_call(
        gather_kernel,
        out_shape=jax.ShapeDtypeStruct((tiles, obs_count, variables + 1, rows_dev, tile_cols), f32),
        in_specs=[smem, smem, vmem, vmem, vmem],
        out_specs=vmem,
        scratch_shapes=[pltpu.VMEM((tiles, variables + 1, tile_rows, tile_cols), f32)],
        compiler_params=pltpu.CompilerParams(vmem_limit_bytes=40 * 1024 * 1024),
    )(slots, rate, coords, values, live)
    depth = (variables + 1) * rows_dev
    held = ((variables + 1 + 7) // 8) * 8
    most = max(lat_count, lon_count, obs_count, 4)
    sides = pl.pallas_call(
        reduce_kernel,
        out_shape=jax.ShapeDtypeStruct((3, rows_dev + 2, held, tile_cols), f32),
        in_specs=[vmem],
        out_specs=vmem,
        scratch_shapes=[
            pltpu.VMEM((lon_count, lat_count * obs_count, depth, tile_cols), f32),
            pltpu.VMEM((lat_count, obs_count, depth, tile_cols), bf16),
            pltpu.VMEM((lat_count, obs_count, depth, tile_cols), bf16),
            pltpu.VMEM((obs_count, depth, tile_cols), f32),
            pltpu.VMEM((obs_count, depth, tile_cols), f32),
            pltpu.VMEM((rows_dev + 2, held, tile_cols), f32),
            pltpu.VMEM((2, rows_dev + 2, held, tile_cols), f32),
            pltpu.SemaphoreType.DMA((4, 2, most)),
        ],
        compiler_params=pltpu.CompilerParams(
            vmem_limit_bytes=40 * 1024 * 1024, collective_id=2, has_side_effects=True
        ),
    )(partial_value.reshape(lon_count, lat_count * obs_count, depth, tile_cols))
    level = variables + 1
    wide = jnp.concatenate(
        [sides[0, :, :level, -1:], sides[1, :, :level], sides[2, :, :level, :1]], axis=2
    )
    grid = sides[1, 1 : rows_dev + 1, :level].transpose(1, 0, 2)
    padded = jnp.einsum("ikj,kc->ijc", wide, w_in, precision=lax.Precision.HIGHEST).astype(
        jnp.bfloat16
    )
    pre = jnp.zeros((rows_dev, tile_cols, channels), jnp.float32)
    for p in range(3):
        for q in range(3):
            pre = pre + jnp.einsum(
                "ijc,cd->ijd",
                padded[p : p + rows_dev, q : q + tile_cols],
                w_conv[p, q],
                preferred_element_type=jnp.float32,
            )
    slope = (
        0.5 * (1.0 + lax.erf(pre * 0.7071067811865476))
        + pre * jnp.exp(-0.5 * pre * pre) * 0.3989422804014327
    )
    grad_pre = (grad_out.astype(jnp.float32) * slope).astype(jnp.bfloat16)
    padded_grad = with_rims(grad_pre)
    terms = []
    back = grad_out.astype(jnp.float32)
    for p in range(3):
        for q in range(3):
            terms.append(
                jnp.einsum(
                    "ijc,ijd->cd",
                    padded[p : p + rows_dev, q : q + tile_cols],
                    grad_pre,
                    preferred_element_type=jnp.float32,
                )
            )
            back = back + jnp.einsum(
                "ijd,cd->ijc",
                padded_grad[2 - p : 2 - p + rows_dev, 2 - q : 2 - q + tile_cols],
                w_conv[p, q],
                preferred_element_type=jnp.float32,
            )
    conv_part = jnp.stack(terms).reshape(3, 3, channels, channels)
    input_part = jnp.einsum("kij,ijc->kc", grid, back, precision=lax.Precision.HIGHEST)
    grad_grid = jnp.einsum(
        "ijc,kc->kij", back, w_in[:variables], precision=lax.Precision.HIGHEST
    ).astype(jnp.bfloat16)
    chunk = conv_part.size // (lat_count * lon_count * obs_count * channels)
    input_part = jnp.pad(input_part, ((0, held - variables - 1), (0, 0)))
    grad_values, grad_in, whole_conv = pl.pallas_call(
        value_kernel,
        out_shape=(
            jax.ShapeDtypeStruct((blocks, variables, width), f32),
            jax.ShapeDtypeStruct((held, channels), f32),
            jax.ShapeDtypeStruct((lon_count, lat_count, obs_count, chunk, channels), bf16),
        ),
        in_specs=[smem, smem, vmem, vmem, vmem, vmem, vmem],
        out_specs=(vmem, vmem, vmem),
        scratch_shapes=[
            pltpu.VMEM((tiles, obs_count, variables * rows_dev, tile_cols), bf16),
            pltpu.VMEM((tiles, variables, tile_rows, tile_cols), f32),
            pltpu.VMEM((held, channels), f32),
            pltpu.VMEM((held, channels), f32),
            pltpu.VMEM((obs_count, held, channels), f32),
            pltpu.VMEM((lat_count, held, channels), f32),
            pltpu.VMEM((lon_count, held, channels), f32),
            pltpu.VMEM((lon_count, lat_count * obs_count, chunk, channels), f32),
            pltpu.VMEM((lat_count, obs_count, chunk, channels), bf16),
            pltpu.VMEM((lat_count, obs_count, chunk, channels), bf16),
            pltpu.VMEM((obs_count, chunk, channels), f32),
            pltpu.VMEM((obs_count, chunk, channels), f32),
            pltpu.VMEM((lon_count, lat_count, obs_count, chunk, channels), bf16),
            pltpu.SemaphoreType.DMA((12, 2, most)),
        ],
        compiler_params=pltpu.CompilerParams(
            vmem_limit_bytes=48 * 1024 * 1024, collective_id=1, has_side_effects=True
        ),
        cost_estimate=pl.CostEstimate(
            flops=4000000000, bytes_accessed=8000000, transcendentals=exps * variables
        ),
    )(
        slots,
        rate,
        coords,
        live,
        grad_grid.reshape(variables * rows_dev, tile_cols),
        input_part,
        conv_part.reshape(lon_count, lat_count * obs_count, chunk, channels),
    )
    grad_in = grad_in[: variables + 1]
    grad_conv = whole_conv.astype(f32).reshape(3, 3, channels, channels)
    return (grad_conv, grad_in, grad_values)


def solution(mesh):
    placed = (
        P(("lat", "lon", "obs"), None, None),
        P(("lat", "lon", "obs"), None, None),
        P(("lat", "lon", "obs"), None),
        P(("lat", "lon", "obs"), None),
        P(),
        P(),
        P(),
        P(("lat", "obs"), "lon", None),
    )
    return jax.shard_map(
        body,
        mesh=mesh,
        in_specs=placed,
        out_specs=(P(), P(), P(("lat", "lon", "obs"), None, None)),
        check_vma=False,
    )
```

```python
import jax
import jax.numpy as jnp
from jax import lax
from jax.experimental import pallas as pl
from jax.experimental.pallas import tpu as pltpu
from jax.sharding import PartitionSpec as P


def with_halo(cells, sides, width):
    for axis, dim in sides:
        count = lax.axis_size(axis)
        head = lax.slice_in_dim(cells, 0, width, axis=dim)
        tail = lax.slice_in_dim(cells, cells.shape[dim] - width, cells.shape[dim], axis=dim)
        cells = jnp.concatenate(
            [
                lax.ppermute(tail, axis, [(i, (i + 1) % count) for i in range(count)]),
                cells,
                lax.ppermute(head, axis, [((i + 1) % count, i) for i in range(count)]),
            ],
            axis=dim,
        )
    return cells


def squares(position, count):
    width = position.shape[1]
    centers = lax.broadcasted_iota(jnp.int32, (count, width), 0).astype(jnp.float32) + 0.5
    diff = centers - position
    return diff * diff


def rates(lengthscale):
    return -1.4426950408889634 / (2.0 * lengthscale * lengthscale)


def each_block(first, last, one):
    together = 4 if first % 4 == 0 and last % 4 == 0 else 1

    def several(m, carry):
        for i in range(together):
            carry = one(m * together + i, carry)
        return carry

    lax.fori_loop(first // together, last // together, several, 0)


def gather_kernel(tile_ref, rate_ref, coords_ref, values_ref, live_ref, out_ref, total):
    variables = values_ref.shape[1]
    tile_rows, tile_cols = total.shape[2:]
    rows_dev = out_ref.shape[3]
    total[...] = jnp.zeros_like(total)

    def one(n, carry):
        t = tile_ref[n]
        place = coords_ref[n].astype(jnp.float32)
        mask = live_ref[pl.ds(n, 1), :].astype(jnp.float32)
        weighted = values_ref[n].astype(jnp.float32) * mask
        row_sq = squares(place[0:1] * tile_rows, tile_rows)
        col_sq = squares(place[1:2] * tile_cols, tile_cols)
        for k in range(variables + 1):
            w = weighted[k : k + 1] if k < variables else mask
            left = (jnp.exp2(row_sq * rate_ref[k]) * w).astype(jnp.bfloat16)
            right = jnp.exp2(col_sq * rate_ref[k]).astype(jnp.bfloat16)
            total[t, k] += lax.dot_general(
                left, right, (((1,), (1,)), ((), ())), preferred_element_type=jnp.float32
            )
        return carry

    each_block(0, coords_ref.shape[0], one)

    def flush(t, carry):
        for o in range(tile_rows // rows_dev):
            for k in range(variables + 1):
                out_ref[t, o, k] = total[t, k, o * rows_dev : (o + 1) * rows_dev]
        return carry

    lax.fori_loop(0, total.shape[0], flush, 0)


def signal_peers(axes, greeted=0):
    barrier = pltpu.get_barrier_semaphore()
    for axis in axes:
        count = lax.axis_size(axis)
        me = lax.axis_index(axis)
        for step in range(1, count):
            pl.semaphore_signal(
                barrier,
                inc=1,
                device_id={axis: lax.rem(me + step, count)},
                device_id_type=pl.DeviceIdType.MESH,
            )
            greeted += 1
    pl.semaphore_wait(barrier, greeted)


def start_copies(axis, source_of, target, sems):
    count = lax.axis_size(axis)
    me = lax.axis_index(axis)
    copies = []
    for step in range(1, count):
        peer = lax.rem(me + step, count)
        copy = pltpu.make_async_remote_copy(
            src_ref=source_of(peer),
            dst_ref=target,
            send_sem=sems.at[0, step],
            recv_sem=sems.at[1, step],
            device_id={axis: peer},
            device_id_type=pl.DeviceIdType.MESH,
        )
        copy.start()
        copies.append(copy)
    return copies


def wait_all(copies):
    for copy in copies:
        copy.wait()


def reduce_kernel(part_ref, out_ref, got1, sum1, got2, sum2, got3, rows, sides, sems):
    lat_count, lon_count, obs_count = (lax.axis_size(a) for a in ("lat", "lon", "obs"))
    lat, lon, obs = (lax.axis_index(a) for a in ("lat", "lon", "obs"))
    rows_dev = rows.shape[0] - 2
    levels = sum1.shape[2] // rows_dev
    mesh_ids = pl.DeviceIdType.MESH
    places = lat_count * obs_count
    place = lat * obs_count + obs
    after = lax.rem(place + 1, places)
    before = lax.rem(place + places - 1, places)
    down = {"lat": after // obs_count, "obs": lax.rem(after, obs_count)}
    up = {"lat": before // obs_count, "obs": lax.rem(before, obs_count)}
    east = {"lon": lax.rem(lon + 1, lon_count)}
    west = {"lon": lax.rem(lon + lon_count - 1, lon_count)}
    rows[...] = jnp.zeros_like(rows)
    barrier = pltpu.get_barrier_semaphore()
    for device in (up, down):
        pl.semaphore_signal(barrier, inc=1, device_id=device, device_id_type=mesh_ids)
    signal_peers(("lat", "lon", "obs"), 2)

    wait_all(start_copies("lon", lambda peer: part_ref.at[peer], got1.at[lon], sems.at[0]))

    def add1(i, carry):
        value = part_ref[lon, i]
        for step in range(1, lon_count):
            value = value + got1[lax.rem(lon + step, lon_count), i]
        sum1[i // obs_count, i % obs_count] = value.astype(jnp.bfloat16)
        return carry

    lax.fori_loop(0, lat_count * obs_count, add1, 0)
    wait_all(start_copies("lat", lambda peer: sum1.at[peer], got2.at[lat], sems.at[1]))

    def add2(i, carry):
        value = sum1[lat, i].astype(jnp.float32)
        for step in range(1, lat_count):
            value = value + got2[lax.rem(lat + step, lat_count), i].astype(jnp.float32)
        sum2[i] = value
        return carry

    lax.fori_loop(0, obs_count, add2, 0)
    wait_all(start_copies("obs", lambda peer: sum2.at[peer], got3.at[obs], sems.at[2]))
    value = sum2[obs]
    for step in range(1, obs_count):
        value = value + got3[lax.rem(obs + step, obs_count)]
    for k in range(levels):
        for r in range(rows_dev):
            rows[r + 1, k : k + 1] = value[k * rows_dev + r : k * rows_dev + r + 1]

    def send(source, target, number, device):
        copy = pltpu.make_async_remote_copy(
            src_ref=source,
            dst_ref=target,
            send_sem=sems.at[3, 0, number],
            recv_sem=sems.at[3, 1, number],
            device_id=device,
            device_id_type=mesh_ids,
        )
        copy.start()
        return copy

    wait_all(
        [
            send(rows.at[1], rows.at[rows_dev + 1], 0, up),
            send(rows.at[rows_dev], rows.at[0], 1, down),
        ]
    )
    rows[0] = rows[0] * (place > 0).astype(jnp.float32)
    rows[rows_dev + 1] = rows[rows_dev + 1] * (place < places - 1).astype(jnp.float32)
    wait_all([send(rows, sides.at[1], 2, west), send(rows, sides.at[0], 3, east)])
    out_ref[0] = sides[0]
    out_ref[1] = rows[...]
    out_ref[2] = sides[1]


def value_kernel(
    slot_ref,
    rate_ref,
    coords_ref,
    live_ref,
    grad_ref,
    input_ref,
    conv_ref,
    out_ref,
    input_out,
    conv_out,
    cells,
    tile_grad,
    own_in1,
    own_in2,
    in1,
    in2,
    in3,
    got1,
    sum1,
    got2,
    sum2,
    got3,
    whole,
    sems,
):
    blocks, variables = out_ref.shape[:2]
    lat_count, lon_count, obs_count = (lax.axis_size(a) for a in ("lat", "lon", "obs"))
    lat, lon, obs = (lax.axis_index(a) for a in ("lat", "lon", "obs"))
    tile_rows, tile_cols = tile_grad.shape[2:]
    rows_dev = tile_rows // obs_count
    signal_peers(("lat", "lon", "obs"))

    reduce1 = start_copies("lon", lambda peer: conv_ref.at[peer], got1.at[lon], sems.at[0])
    home = lon * lat_count + lat
    cells[home, obs] = grad_ref[...]
    in1[obs] = input_ref[...]
    mine = cells.at[home, obs]
    gather1 = start_copies("obs", lambda peer: mine, mine, sems.at[1])
    gather1 += start_copies("obs", lambda peer: input_ref, in1.at[obs], sems.at[2])
    wait_all(gather1)
    total = jnp.sum(in1[...], axis=0)
    own_in1[...] = total
    in2[lat] = total
    gather2 = start_copies("lat", lambda peer: cells.at[home], cells.at[home], sems.at[3])
    gather2 += start_copies("lat", lambda peer: own_in1, in2.at[lat], sems.at[4])

    wait_all(reduce1)

    def add1(i, carry):
        value = conv_ref[lon, i]
        for step in range(1, lon_count):
            value = value + got1[lax.rem(lon + step, lon_count), i]
        sum1[i // obs_count, i % obs_count] = value.astype(jnp.bfloat16)
        return carry

    lax.fori_loop(0, lat_count * obs_count, add1, 0)
    reduce2 = start_copies("lat", lambda peer: sum1.at[peer], got2.at[lat], sems.at[5])
    wait_all(gather2)
    total = jnp.sum(in2[...], axis=0)
    own_in2[...] = total
    in3[lon] = total
    group = pl.ds(lon * lat_count, lat_count)
    gather3 = start_copies("lon", lambda peer: cells.at[group], cells.at[group], sems.at[6])
    gather3 += start_copies("lon", lambda peer: own_in2, in3.at[lon], sems.at[7])
    wait_all(gather3)
    input_out[...] = jnp.sum(in3[...], axis=0)

    def spread(t, carry):
        for o in range(obs_count):
            piece = cells[t, o].astype(jnp.float32)
            for k in range(variables):
                tile_grad[t, k, o * rows_dev : (o + 1) * rows_dev] = piece[
                    k * rows_dev : (k + 1) * rows_dev
                ]
        return carry

    lax.fori_loop(0, tile_grad.shape[0], spread, 0)

    def one(n, carry):
        t = slot_ref[n]
        place = coords_ref[n].astype(jnp.float32)
        mask = live_ref[pl.ds(n, 1), :].astype(jnp.float32)
        row_sq = squares(place[0:1] * tile_rows, tile_rows)
        col_sq = squares(place[1:2] * tile_cols, tile_cols)
        for k in range(variables):
            left = jnp.exp2(row_sq * rate_ref[k])
            right = jnp.exp2(col_sq * rate_ref[k]).astype(jnp.bfloat16)
            middle = jnp.dot(
                tile_grad[t, k].astype(jnp.bfloat16), right, preferred_element_type=jnp.float32
            )
            out_ref[n, k : k + 1] = jnp.sum(left * middle, axis=0, keepdims=True) * mask
        return carry

    def some(first, last):
        each_block(first * blocks // 64, last * blocks // 64, one)

    some(0, 8)
    wait_all(reduce2)

    def add2(i, carry):
        value = sum1[lat, i].astype(jnp.float32)
        for step in range(1, lat_count):
            value = value + got2[lax.rem(lat + step, lat_count), i].astype(jnp.float32)
        sum2[i] = value
        return carry

    lax.fori_loop(0, obs_count, add2, 0)
    reduce3 = start_copies("obs", lambda peer: sum2.at[peer], got3.at[obs], sems.at[8])
    some(8, 24)
    wait_all(reduce3)
    value = sum2[obs]
    for step in range(1, obs_count):
        value = value + got3[lax.rem(obs + step, obs_count)]
    whole[lon, lat, obs] = value.astype(jnp.bfloat16)
    mine1 = whole.at[lon, lat, obs]
    spread1 = start_copies("obs", lambda peer: mine1, mine1, sems.at[9])
    some(24, 36)
    wait_all(spread1)
    mine2 = whole.at[lon, lat]
    spread2 = start_copies("lat", lambda peer: mine2, mine2, sems.at[10])
    some(36, 52)
    wait_all(spread2)
    mine3 = whole.at[lon]
    spread3 = start_copies("lon", lambda peer: mine3, mine3, sems.at[11])
    some(52, 64)
    wait_all(spread3)

    def give(i, carry):
        a, b = i // lat_count, i % lat_count
        for o in range(obs_count):
            conv_out[a, b, o] = whole[a, b, o]
        return carry

    lax.fori_loop(0, lon_count * lat_count, give, 0)


def with_rims(field):
    padded = with_halo(field, ((("lat", "obs"), 0), ("lon", 1)), 1)
    place = lax.axis_index("lat") * lax.axis_size("obs") + lax.axis_index("obs")
    last_place = lax.axis_size("lat") * lax.axis_size("obs") - 1
    row_ids = jnp.arange(padded.shape[0])
    keep = jnp.where(
        row_ids == 0, place > 0, jnp.where(row_ids == padded.shape[0] - 1, place < last_place, True)
    )
    return padded * keep[:, None, None].astype(padded.dtype)


def body(coords, values, live, tile_of, lengthscale, w_in, w_conv, grad_out):
    lat_count = lax.axis_size("lat")
    lon_count = lax.axis_size("lon")
    obs_count = lax.axis_size("obs")
    tiles = lat_count * lon_count
    blocks = coords.shape[0]
    width = coords.shape[2]
    variables = values.shape[1]
    rows_dev, tile_cols, channels = grad_out.shape
    tile_rows = rows_dev * obs_count
    everyone = ("lat", "lon", "obs")
    rate = rates(lengthscale)
    target = tile_of[:, 0]
    smem = pl.BlockSpec(memory_space=pltpu.SMEM)
    vmem = pl.BlockSpec(memory_space=pltpu.VMEM)
    exps = blocks * width * (tile_rows + tile_cols)
    f32, bf16 = jnp.float32, jnp.bfloat16
    slots = (target % lon_count) * lat_count + target // lon_count
    partial_value = pl.pallas_call(
        gather_kernel,
        out_shape=jax.ShapeDtypeStruct((tiles, obs_count, variables + 1, rows_dev, tile_cols), f32),
        in_specs=[smem, smem, vmem, vmem, vmem],
        out_specs=vmem,
        scratch_shapes=[pltpu.VMEM((tiles, variables + 1, tile_rows, tile_cols), f32)],
        compiler_params=pltpu.CompilerParams(vmem_limit_bytes=40 * 1024 * 1024),
    )(slots, rate, coords, values, live)
    depth = (variables + 1) * rows_dev
    held = ((variables + 1 + 7) // 8) * 8
    most = max(lat_count, lon_count, obs_count, 4)
    sides = pl.pallas_call(
        reduce_kernel,
        out_shape=jax.ShapeDtypeStruct((3, rows_dev + 2, held, tile_cols), f32),
        in_specs=[vmem],
        out_specs=vmem,
        scratch_shapes=[
            pltpu.VMEM((lon_count, lat_count * obs_count, depth, tile_cols), f32),
            pltpu.VMEM((lat_count, obs_count, depth, tile_cols), bf16),
            pltpu.VMEM((lat_count, obs_count, depth, tile_cols), bf16),
            pltpu.VMEM((obs_count, depth, tile_cols), f32),
            pltpu.VMEM((obs_count, depth, tile_cols), f32),
            pltpu.VMEM((rows_dev + 2, held, tile_cols), f32),
            pltpu.VMEM((2, rows_dev + 2, held, tile_cols), f32),
            pltpu.SemaphoreType.DMA((4, 2, most)),
        ],
        compiler_params=pltpu.CompilerParams(
            vmem_limit_bytes=40 * 1024 * 1024, collective_id=2, has_side_effects=True
        ),
    )(partial_value.reshape(lon_count, lat_count * obs_count, depth, tile_cols))
    level = variables + 1
    wide = jnp.concatenate(
        [sides[0, :, :level, -1:], sides[1, :, :level], sides[2, :, :level, :1]], axis=2
    )
    grid = sides[1, 1 : rows_dev + 1, :level].transpose(1, 0, 2)
    padded = jnp.einsum("ikj,kc->ijc", wide, w_in, precision=lax.Precision.HIGHEST).astype(
        jnp.bfloat16
    )
    pre = jnp.zeros((rows_dev, tile_cols, channels), jnp.float32)
    for p in range(3):
        for q in range(3):
            pre = pre + jnp.einsum(
                "ijc,cd->ijd",
                padded[p : p + rows_dev, q : q + tile_cols],
                w_conv[p, q],
                preferred_element_type=jnp.float32,
            )
    slope = (
        0.5 * (1.0 + lax.erf(pre * 0.7071067811865476))
        + pre * jnp.exp(-0.5 * pre * pre) * 0.3989422804014327
    )
    grad_pre = (grad_out.astype(jnp.float32) * slope).astype(jnp.bfloat16)
    padded_grad = with_rims(grad_pre)
    terms = []
    back = grad_out.astype(jnp.float32)
    for p in range(3):
        for q in range(3):
            terms.append(
                jnp.einsum(
                    "ijc,ijd->cd",
                    padded[p : p + rows_dev, q : q + tile_cols],
                    grad_pre,
                    preferred_element_type=jnp.float32,
                )
            )
            back = back + jnp.einsum(
                "ijd,cd->ijc",
                padded_grad[2 - p : 2 - p + rows_dev, 2 - q : 2 - q + tile_cols],
                w_conv[p, q],
                preferred_element_type=jnp.float32,
            )
    conv_part = jnp.stack(terms).reshape(3, 3, channels, channels)
    input_part = jnp.einsum("kij,ijc->kc", grid, back, precision=lax.Precision.HIGHEST)
    grad_grid = jnp.einsum(
        "ijc,kc->kij", back, w_in[:variables], precision=lax.Precision.HIGHEST
    ).astype(jnp.bfloat16)
    chunk = conv_part.size // (lat_count * lon_count * obs_count * channels)
    input_part = jnp.pad(input_part, ((0, held - variables - 1), (0, 0)))
    grad_values, grad_in, whole_conv = pl.pallas_call(
        value_kernel,
        out_shape=(
            jax.ShapeDtypeStruct((blocks, variables, width), f32),
            jax.ShapeDtypeStruct((held, channels), f32),
            jax.ShapeDtypeStruct((lon_count, lat_count, obs_count, chunk, channels), bf16),
        ),
        in_specs=[smem, smem, vmem, vmem, vmem, vmem, vmem],
        out_specs=(vmem, vmem, vmem),
        scratch_shapes=[
            pltpu.VMEM((tiles, obs_count, variables * rows_dev, tile_cols), bf16),
            pltpu.VMEM((tiles, variables, tile_rows, tile_cols), f32),
            pltpu.VMEM((held, channels), f32),
            pltpu.VMEM((held, channels), f32),
            pltpu.VMEM((obs_count, held, channels), f32),
            pltpu.VMEM((lat_count, held, channels), f32),
            pltpu.VMEM((lon_count, held, channels), f32),
            pltpu.VMEM((lon_count, lat_count * obs_count, chunk, channels), f32),
            pltpu.VMEM((lat_count, obs_count, chunk, channels), bf16),
            pltpu.VMEM((lat_count, obs_count, chunk, channels), bf16),
            pltpu.VMEM((obs_count, chunk, channels), f32),
            pltpu.VMEM((obs_count, chunk, channels), f32),
            pltpu.VMEM((lon_count, lat_count, obs_count, chunk, channels), bf16),
            pltpu.SemaphoreType.DMA((12, 2, most)),
        ],
        compiler_params=pltpu.CompilerParams(
            vmem_limit_bytes=48 * 1024 * 1024, collective_id=1, has_side_effects=True
        ),
        cost_estimate=pl.CostEstimate(
            flops=4000000000, bytes_accessed=8000000, transcendentals=exps * variables
        ),
    )(
        slots,
        rate,
        coords,
        live,
        grad_grid.reshape(variables * rows_dev, tile_cols),
        input_part,
        conv_part.reshape(lon_count, lat_count * obs_count, chunk, channels),
    )
    grad_in = grad_in[: variables + 1]
    grad_conv = whole_conv.astype(f32).reshape(3, 3, channels, channels)
    return (grad_conv, grad_in, grad_values)


def solution(mesh):
    placed = (
        P(("lat", "lon", "obs"), None, None),
        P(("lat", "lon", "obs"), None, None),
        P(("lat", "lon", "obs"), None),
        P(("lat", "lon", "obs"), None),
        P(),
        P(),
        P(),
        P(("lat", "obs"), "lon", None),
    )
    return jax.shard_map(
        body,
        mesh=mesh,
        in_specs=placed,
        out_specs=(P(), P(), P(("lat", "lon", "obs"), None, None)),
        check_vma=False,
    )
```
